512 devices in a mesh: lvl: 128 (over z, x, core), row: 4 (over y).
Axes of the slice: x: 4, y: 4, z: 16, core: 2. Of those that a mesh axis runs over, the one named last changes fastest.
Arguments:
- right_side: bfloat16 [7168, 64, 128], P(('lvl', 'row')), may hold values from -4 to 4
- factor_blocks: bfloat16 [7168, 3, 64, 64], P(('lvl', 'row')), may hold values from -0.3125 to 0.3125
- diag_inverse: bfloat16 [7168, 64, 64], P(('lvl', 'row')), may hold values from -1 to 2.5
- pattern: int32 [7168, 3], P(('lvl', 'row')), may hold values from 0 to 41, as said below
Outputs:
- forward_solution: bfloat16 [7168, 64, 128], P(('lvl', 'row'))
- backward_solution: bfloat16 [7168, 64, 128], P(('lvl', 'row'))
The draws below stay inside these ranges and needn't reach their ends.
Inputs may be any that keep to these rules, and one draw needn't show every extreme that they name: `pattern`: entries of block rows of level 0 are not used. For a block row of rank 0 every entry is at least 14; for a block row of the last rank, 63, every entry is below 28.
All inputs are finite; a program needn't handle non-finite values.
Results may differ from the reference program's by a relative error of at most 0.02.
Values may be sent and summed in bfloat16 or wider, within the bound.
No kernel may reach another device: no remote copies, remote signals or barrier semaphores. Data moves between devices by JAX's collectives and lax.ppermute only.
A program may use at most 64 MiB of HBM per device.

```python
import jax
import jax.numpy as jnp
from jax import lax

BS = 64
RHS = 128
NB = 14
K = 3
LEVELS = 8
ROWS = 7168
SKIP = 1344


def draw_pattern(key, part):
    key = jax.random.fold_in(key, 1)
    per_level = ROWS // LEVELS
    rank_count = per_level // NB
    row_ids = jnp.arange(ROWS, dtype=jnp.int32)
    order_ids = (row_ids + SKIP) % ROWS
    row_rank = order_ids % per_level // NB
    slot_index = row_ids % NB
    lower_bound = jnp.where(row_rank == 0, NB, 0)
    upper_bound = jnp.where(row_rank == rank_count - 1, 2 * NB, 3 * NB)
    raw_values = jax.random.randint(key, (ROWS, K), 0, 3 * NB)
    column_ids = lower_bound[:, None] + raw_values % (upper_bound - lower_bound)[:, None]
    first_entry = (jnp.arange(K, dtype=jnp.int32) == 0)[None, :]
    column_ids = jnp.where((slot_index == 0)[:, None] & first_entry, (upper_bound - 1)[:, None], column_ids)
    column_ids = jnp.where((slot_index == 1)[:, None] & first_entry, lower_bound[:, None], column_ids)
    return column_ids.astype(jnp.int32)


def draw_diag_inverse(key, part):
    key = jax.random.fold_in(key, 2)
    noise_key, scale_key = jax.random.split(key)
    identity = jnp.eye(BS, dtype=jnp.float32)
    noise = jnp.clip(jax.random.normal(noise_key, (ROWS, BS, BS), jnp.float32), -4.0, 4.0) * 0.35 / 8.0
    scales = jnp.exp(jax.random.uniform(scale_key, (ROWS, BS, 1), jnp.float32, jnp.log(0.5), jnp.log(2.0)))
    return (noise + identity[None] * scales).astype(jnp.bfloat16)


def draw_right_side(key, part):
    key = jax.random.fold_in(key, 3)
    per_level = ROWS // LEVELS
    row_ids = jnp.arange(ROWS, dtype=jnp.int32)
    first_level = (row_ids + SKIP) % ROWS < per_level
    row_scale = jnp.where(first_level, 1.0, 0.25).astype(jnp.float32)[:, None, None]
    values = jnp.clip(jax.random.normal(key, (ROWS, BS, RHS), jnp.float32), -4.0, 4.0)
    return (values * row_scale).astype(jnp.bfloat16)


def block_scale(rng, dims, shards, low, largest):
    def one(dim, shards_of):
        draws = jax.random.uniform(jax.random.fold_in(jax.random.fold_in(rng, 6), dim), (shards_of,), jnp.float32, low / len(shards), largest / len(shards))
        return jnp.repeat(jnp.exp(draws), dims[dim] // shards_of).reshape((-1,) + (1,) * (len(dims) - dim - 1))

    gain = one(*shards[0])
    for cut in shards[1:]:
        gain = gain * one(*cut)
    return gain


def gaussian(stream_key, dims, width, most, cuts=(), kind=jnp.bfloat16):
    values = jax.random.normal(stream_key, dims, jnp.float32) * width
    if len(cuts) > 0:
        values = block_scale(stream_key, dims, cuts, -0.22, 0.18) * values
    return jnp.clip(values, min=-most, max=most).astype(kind)


def setup_inputs(seed: int = 0) -> dict:
    arg_keys = jax.random.split(jax.random.key(seed), 5)
    right_side = draw_right_side(jax.random.fold_in(arg_keys[4], 71), 0)
    factor_blocks = gaussian(arg_keys[1], (ROWS, K, BS, BS), (5 * BS) ** -0.5, 0.3125, ((0, 512),))
    diag_inverse = draw_diag_inverse(jax.random.fold_in(arg_keys[4], 71), 0)
    pattern = draw_pattern(jax.random.fold_in(arg_keys[4], 71), 0)
    return {"right_side": right_side, "factor_blocks": factor_blocks, "diag_inverse": diag_inverse, "pattern": pattern}


def level_order(right_side, factor_blocks, diag_inverse, pattern):
    per_level = ROWS // LEVELS
    local_rows = jnp.arange(per_level, dtype=jnp.int32)
    owner_rank = local_rows // NB
    forward_solution = jnp.zeros((ROWS, BS, RHS), jnp.bfloat16)
    for level_index in range(LEVELS):
        first_row = level_index * per_level
        last_row = first_row + per_level
        residual = right_side[first_row:last_row].astype(jnp.float32)
        if level_index > 0:
            pattern_rows = pattern[first_row:last_row]
            source = (level_index - 1) * per_level + (owner_rank[:, None] + pattern_rows // NB - 1) * NB + pattern_rows % NB
            picked = forward_solution[source.astype(jnp.int32)].astype(jnp.float32)
            coupled = jnp.einsum("nkab,nkbw->naw", factor_blocks[first_row:last_row].astype(jnp.float32), picked)
            residual = residual - coupled
        reduced = lax.optimization_barrier(residual.astype(jnp.bfloat16))
        solved_now = jnp.einsum("nab,nbw->naw", diag_inverse[first_row:last_row].astype(jnp.float32), reduced.astype(jnp.float32))
        forward_solution = forward_solution.at[first_row:last_row].set(solved_now.astype(jnp.bfloat16))
    ranks = per_level // NB
    key_count = ranks * 3 * NB
    all_keys = jnp.arange(key_count, dtype=jnp.int32)
    key_owner = all_keys // (3 * NB)
    key_place = all_keys % (3 * NB)
    target_rank = key_owner + key_place // NB - 1
    in_group = (target_rank >= 0) & (target_rank < ranks)
    target_row = target_rank * NB + key_place % NB
    target_row = jnp.where(in_group, target_row, per_level).astype(jnp.int32)
    backward_solution = jnp.zeros((ROWS, BS, RHS), jnp.bfloat16)
    for level_index in reversed(range(LEVELS)):
        first_row = level_index * per_level
        last_row = first_row + per_level
        residual = forward_solution[first_row:last_row].astype(jnp.float32)
        if level_index < LEVELS - 1:
            above = backward_solution[last_row:last_row + per_level].astype(jnp.float32)
            products = jnp.einsum("nkba,nbw->nkaw", factor_blocks[last_row:last_row + per_level].astype(jnp.float32), above)
            pattern_rows = pattern[last_row:last_row + per_level]
            key_index = (owner_rank[:, None] * (3 * NB) + pattern_rows).astype(jnp.int32)
            partial_value = jax.ops.segment_sum(products.reshape(per_level * K, BS * RHS), key_index.reshape(-1), num_segments=key_count)
            partial_value = lax.optimization_barrier(partial_value.astype(jnp.bfloat16)).astype(jnp.float32)
            incoming = jax.ops.segment_sum(partial_value, target_row, num_segments=per_level + 1)[:per_level]
            residual = residual - incoming.reshape(per_level, BS, RHS)
        reduced = lax.optimization_barrier(residual.astype(jnp.bfloat16))
        solved_now = jnp.einsum("nba,nbw->naw", diag_inverse[first_row:last_row].astype(jnp.float32), reduced.astype(jnp.float32))
        backward_solution = backward_solution.at[first_row:last_row].set(solved_now.astype(jnp.bfloat16))
    return forward_solution, backward_solution


def reference(right_side, factor_blocks, diag_inverse, pattern):
    forward_solution, backward_solution = level_order(
        jnp.roll(right_side, SKIP, axis=0),
        jnp.roll(factor_blocks, SKIP, axis=0),
        jnp.roll(diag_inverse, SKIP, axis=0),
        jnp.roll(pattern, SKIP, axis=0))
    return jnp.roll(forward_solution, -SKIP, axis=0), jnp.roll(backward_solution, -SKIP, axis=0)
```

```python
import functools

import jax
import jax.numpy as jnp
from jax import lax
from jax.experimental import pallas as pl
from jax.experimental.pallas import tpu as pltpu
from jax.sharding import PartitionSpec as P

LEVELS = 8
RANKS = 64
SLOTS = 14
PAIRS = 7
LINKS = 3
ORDER = 64
COLS = 128
PART = 16
ROTATION = 96
W_ROWS = SLOTS * ORDER
W_ALL = W_ROWS + 16
AXES = ("lvl", "row")
BF16 = jnp.bfloat16
F32 = jnp.float32
VMEM = pltpu.VMEM


def place(rank, slot):
    plane, side = divmod(rank, 4)
    y = side if plane % 2 == 0 else 3 - side
    return (plane * 8 + slot) * 4 + y


def gather_pairs():
    pairs = []
    for device in range(LEVELS * RANKS):
        level, rank = divmod((device + ROTATION) % (LEVELS * RANKS), RANKS)
        pairs.append((device, place(rank, level)))
    return pairs


def neighbour_pairs(step):
    return [
        (place(rank, slot), place(rank + step, slot))
        for rank in range(RANKS)
        if 0 <= rank + step < RANKS
        for slot in range(LEVELS)
    ]


def group_list():
    return [[plane * 8 + slot for slot in range(8)] for plane in range(16)]


def left_lanes(shape):
    return lax.broadcasted_iota(jnp.int32, shape, len(shape) - 1) < ORDER


def call(kernel, outs, operands, in_specs, scratch=(), flops=0):
    return pl.pallas_call(
        kernel,
        out_shape=[jax.ShapeDtypeStruct(shape, dtype) for shape, dtype in outs],
        grid=(1,),
        in_specs=in_specs,
        out_specs=[
            pl.BlockSpec(shape, functools.partial(lambda n, i: (0,) * n, len(shape)))
            for shape, _ in outs
        ],
        scratch_shapes=list(scratch),
        compiler_params=pltpu.CompilerParams(vmem_limit_bytes=32 * 1024 * 1024),
    )(*operands)


def whole(array):
    return pl.BlockSpec(array.shape, lambda i: (0,) * array.ndim)


def at_level(level, rows, width):
    return pl.BlockSpec((1, rows, width), lambda i: (level, 0, 0))


def prepare_kernel(first_ref, rhs_ref, factor_ref, diag_ref, pattern_ref, w_ref, rhs_t_ref):
    first = first_ref[0] == 1
    for i in range(PAIRS):
        halves = []
        for n, side in ((i, 0), (i + PAIRS, 1)):
            blocks = [factor_ref[n, m] for m in range(LINKS)]
            diag = diag_ref[n]
            tail = [diag, blocks[2]] if side == 0 else [blocks[2], diag]
            w_ref[n * ORDER : (n + 1) * ORDER, :] = jnp.concatenate(blocks[:2] + tail, axis=1)
            rhs = rhs_ref[n]
            solved = jnp.dot(diag, rhs, preferred_element_type=F32).astype(BF16)
            halves.append(jnp.where(first, solved, rhs))
        both = jnp.concatenate(halves, axis=0).astype(F32)
        turned = both.T.astype(BF16)
        for j in range(COLS // PART):
            rhs_t_ref[j, i] = turned[j * PART : (j + 1) * PART, :]
    w_ref[W_ROWS:, :] = pattern_ref[...]


def finish_kernel(parts_ref, out_ref):
    for i in range(PAIRS):
        columns = jnp.concatenate([parts_ref[j, i] for j in range(COLS // PART)], axis=0)
        turned = columns.astype(F32).T.astype(BF16)
        out_ref[i] = turned[:ORDER]
        out_ref[i + PAIRS] = turned[ORDER:]


def put_window(window_ref, source_ref, base):
    for i in range(PAIRS):
        pair = source_ref[i].astype(F32)
        swapped = pltpu.roll(pair, ORDER, 1)
        left = left_lanes(pair.shape)
        window_ref[base + i] = jnp.where(left, pair, swapped).astype(BF16)
        window_ref[base + PAIRS + i] = jnp.where(left, swapped, pair).astype(BF16)


def diag_pair(w_ref, i):
    upper = w_ref[0, i * ORDER : (i + 1) * ORDER, 128:]
    j = i + PAIRS
    lower = w_ref[0, j * ORDER : (j + 1) * ORDER, 128:]
    left = left_lanes(upper.shape)
    zero = jnp.zeros_like(upper)
    return jnp.concatenate([jnp.where(left, upper, zero), jnp.where(left, zero, lower)], axis=0)


def picked_product(pattern_ref, w_ref, window_ref, level, n):
    p = [pattern_ref[level, LINKS * n + m] for m in range(LINKS)]
    a, b, c = (window_ref[index] for index in p)
    left = left_lanes(a.shape)
    zero = jnp.zeros_like(c)
    head = jnp.where(left, a, b)
    tail = jnp.where(left, zero, c) if n < PAIRS else jnp.where(left, c, zero)
    w = w_ref[0, n * ORDER : (n + 1) * ORDER, :]
    return lax.dot_general(
        jnp.concatenate([head, tail], axis=1), w, (((1,), (1,)), ((), ())), preferred_element_type=F32
    )


def forward_pair(pattern_ref, w_ref, window_ref, rhs_ref, level, i):
    coupled = jnp.concatenate(
        [picked_product(pattern_ref, w_ref, window_ref, level, n) for n in (i, i + PAIRS)], axis=1
    )
    reduced = (rhs_ref[0, i].astype(F32) - coupled).astype(BF16)
    return lax.dot_general(
        reduced, diag_pair(w_ref, i), (((1,), (1,)), ((), ())), preferred_element_type=F32
    ).astype(BF16)


def fill_window(window_ref, own_ref, below_ref, above_ref):
    put_window(window_ref, below_ref, 0)
    put_window(window_ref, own_ref, SLOTS)
    put_window(window_ref, above_ref, 2 * SLOTS)


def forward_kernel(level, pattern_ref, w_ref, rhs_ref, own_ref, below_ref, above_ref, out_ref, window_ref):
    fill_window(window_ref, own_ref, below_ref, above_ref)
    for i in range(PAIRS):
        out_ref[i] = forward_pair(pattern_ref, w_ref, window_ref, rhs_ref, level, i)


def spread(pattern_ref, w_ref, solved, level, sums_ref, total_ref):
    for q in range(LINKS * SLOTS):
        total_ref[q] = jnp.zeros(total_ref.shape[1:], F32)
    for i in range(PAIRS):
        j = i + PAIRS
        left = left_lanes(solved[i].shape)
        zero = jnp.zeros_like(solved[i])
        rows = jnp.concatenate(
            [jnp.where(left, solved[i], zero), jnp.where(left, zero, solved[i])], axis=0
        )
        w = jnp.concatenate(
            [w_ref[0, n * ORDER : (n + 1) * ORDER, :] for n in (i, j)], axis=0
        )
        products = jnp.dot(rows, w, preferred_element_type=F32)
        for n, product in ((i, products[:PART]), (j, products[PART:])):
            head, tail = product[:, :128], product[:, 128:]
            left = left_lanes(head.shape)
            zero = jnp.zeros_like(head)
            terms = (
                jnp.where(left, head, zero),
                jnp.where(left, zero, head),
                jnp.where(left, zero, tail) if n < PAIRS else jnp.where(left, tail, zero),
            )
            for m in range(LINKS):
                q = pattern_ref[level, LINKS * n + m]
                total_ref[q] += terms[m]
    for part in range(LINKS):
        for i in range(PAIRS):
            one = total_ref[part * SLOTS + i]
            two = total_ref[part * SLOTS + PAIRS + i]
            left = left_lanes(one.shape)
            one = one + pltpu.roll(one, ORDER, 1)
            two = two + pltpu.roll(two, ORDER, 1)
            sums_ref[part, i] = jnp.where(left, one, two).astype(BF16)


def backward_pair(w_ref, reduced, i):
    return jnp.dot(reduced, diag_pair(w_ref, i), preferred_element_type=F32).astype(BF16)


def turn_kernel(
    level, pattern_ref, w_ref, rhs_ref, own_ref, below_ref, above_ref,
    out_ref, back_ref, sums_ref, window_ref, total_ref,
):
    fill_window(window_ref, own_ref, below_ref, above_ref)
    solved = []
    for i in range(PAIRS):
        forward = forward_pair(pattern_ref, w_ref, window_ref, rhs_ref, level, i)
        out_ref[i] = forward
        back = backward_pair(w_ref, forward, i)
        back_ref[i] = back
        solved.append(back)
    spread(pattern_ref, w_ref, solved, level, sums_ref, total_ref)


def backward_solve(w_ref, forward_ref, own_ref, below_ref, above_ref, back_ref):
    solved = []
    for i in range(PAIRS):
        incoming = (
            own_ref[1, i].astype(F32) + below_ref[i].astype(F32) + above_ref[i].astype(F32)
        )
        reduced = (forward_ref[i].astype(F32) - incoming).astype(BF16)
        back = backward_pair(w_ref, reduced, i)
        back_ref[i] = back
        solved.append(back)
    return solved


def backward_kernel(
    level, pattern_ref, w_ref, forward_ref, own_ref, below_ref, above_ref, back_ref, sums_ref, total_ref
):
    solved = backward_solve(w_ref, forward_ref, own_ref, below_ref, above_ref, back_ref)
    spread(pattern_ref, w_ref, solved, level, sums_ref, total_ref)


def last_kernel(w_ref, forward_ref, own_ref, below_ref, above_ref, back_ref):
    backward_solve(w_ref, forward_ref, own_ref, below_ref, above_ref, back_ref)


def per_device(right_side, factor_blocks, diag_inverse, pattern):
    to_group = gather_pairs()
    to_native = [(b, a) for a, b in to_group]
    up, down = neighbour_pairs(1), neighbour_pairs(-1)
    groups = group_list()
    smem = pl.BlockSpec(memory_space=pltpu.SMEM)
    solved_shape = ((PAIRS, PART, 128), BF16)
    window = VMEM((LINKS * SLOTS, PART, 128), BF16)
    total = VMEM((LINKS * SLOTS, PART, 128), F32)

    device = lax.axis_index("lvl") * 4 + lax.axis_index("row")
    own_level = (device + ROTATION) % (LEVELS * RANKS) // RANKS
    first = (own_level == 0).astype(jnp.int32).reshape(1)
    entries = jnp.clip(pattern, 0, LINKS * SLOTS - 1).astype(BF16).reshape(1, LINKS * SLOTS)
    entries = jnp.pad(entries, ((0, 15), (0, 256 - LINKS * SLOTS)))

    factors, rhs = call(
        prepare_kernel,
        [((W_ALL, 256), BF16), ((COLS // PART, PAIRS, PART, 128), BF16)],
        (first, right_side, factor_blocks, diag_inverse, entries),
        [smem, whole(right_side), whole(factor_blocks), whole(diag_inverse), whole(entries)],
    )
    factors = lax.ppermute(factors, AXES, to_group)
    rhs = lax.ppermute(rhs, AXES, to_group)
    factors = lax.all_gather(factors, "lvl", axis_index_groups=groups)
    rhs = lax.all_to_all(rhs, "lvl", 0, 0, axis_index_groups=groups)
    patterns = factors[:, W_ROWS, : LINKS * SLOTS].astype(jnp.int32)

    def exchange(to_above, to_below):
        return lax.ppermute(to_above, AXES, up), lax.ppermute(to_below, AXES, down)

    small = pl.BlockSpec((PAIRS, PART, 128), lambda i: (0, 0, 0))
    sums_spec = pl.BlockSpec((LINKS, PAIRS, PART, 128), lambda i: (0, 0, 0, 0))
    sums_shape = ((LINKS, PAIRS, PART, 128), BF16)

    def rhs_spec(level):
        return pl.BlockSpec((1, PAIRS, PART, 128), lambda i: (level, 0, 0, 0))

    latest = rhs[0]
    forward = [latest]
    for level in range(1, LEVELS - 1):
        below, above = exchange(latest, latest)
        (latest,) = call(
            functools.partial(forward_kernel, level),
            [solved_shape],
            (patterns, factors, rhs, latest, below, above),
            [smem, at_level(level, W_ALL, 256), rhs_spec(level), small, small, small],
            [window],
        )
        forward.append(latest)
    below, above = exchange(latest, latest)
    level = LEVELS - 1
    latest, back, sums = call(
        functools.partial(turn_kernel, level),
        [solved_shape, solved_shape, sums_shape],
        (patterns, factors, rhs, latest, below, above),
        [smem, at_level(level, W_ALL, 256), rhs_spec(level), small, small, small],
        [window, total],
    )
    forward.append(latest)
    backward = [back]
    for level in range(LEVELS - 2, 0, -1):
        below, above = exchange(sums[2], sums[0])
        back, sums = call(
            functools.partial(backward_kernel, level),
            [solved_shape, sums_shape],
            (patterns, factors, forward[level], sums, below, above),
            [smem, at_level(level, W_ALL, 256), small, sums_spec, small, small],
            [total],
        )
        backward.append(back)
    below, above = exchange(sums[2], sums[0])
    (back,) = call(
        last_kernel,
        [solved_shape],
        (factors, forward[0], sums, below, above),
        [at_level(0, W_ALL, 256), small, sums_spec, small, small],
    )
    backward.append(back)

    def to_output(levels):
        parts = lax.all_to_all(jnp.stack(levels), "lvl", 0, 0, axis_index_groups=groups)
        parts = lax.ppermute(parts, AXES, to_native)
        (out,) = call(
            finish_kernel, [((SLOTS, ORDER, COLS), BF16)], (parts,), [whole(parts)]
        )
        return out

    return to_output(forward), to_output(backward[::-1])


def solution(mesh):
    return jax.shard_map(
        per_device,
        mesh=mesh,
        in_specs=(
            P(AXES, None, None),
            P(AXES, None, None, None),
            P(AXES, None, None),
            P(AXES, None),
        ),
        out_specs=(P(AXES, None, None), P(AXES, None, None)),
        check_vma=False,
    )
```

```python
import functools

import jax
import jax.numpy as jnp
from jax import lax
from jax.experimental import pallas as pl
from jax.experimental.pallas import tpu as pltpu
from jax.sharding import PartitionSpec as P

LEVELS = 8
RANKS = 64
SLOTS = 14
PAIRS = 7
LINKS = 3
ORDER = 64
COLS = 128
PART = 16
WINDOW = LINKS * SLOTS
ROTATION = 96
PLANES = 16
ROWS = PAIRS * ORDER
BLOCK = ROWS + 16
SHARD = LINKS * BLOCK
PIECE = PAIRS * 16
WIDE = 2 * LINKS * ORDER
CHUNK = LEVELS // 2
AXES = ("lvl", "row")
BF16 = jnp.bfloat16
F32 = jnp.float32
VMEM = pltpu.VMEM

PLANE_OF = [(band + 14) % PLANES for band in range(PLANES)]


def slot_of(band, turn):
    return (turn - band) % 4 * 2 + turn // 4


def turn_of_slot(slot, shift):
    return (slot // 2 + shift) % 4 + slot % 2 * 4


def place_slot(rank, slot):
    band, side = divmod(rank, 4)
    y = side if band % 2 == 0 else 3 - side
    return (PLANE_OF[band] * 8 + slot) * 4 + y


def place(rank, turn):
    return place_slot(rank, slot_of(rank // 4, turn))


def native(level, rank):
    return (level * RANKS + rank - ROTATION) % (LEVELS * RANKS)


def level_pairs():
    return [
        (native(level, rank), place(rank, level))
        for level in range(LEVELS)
        for rank in range(RANKS)
    ]


def neighbour_pairs(step):
    return [
        (place_slot(rank, slot), place_slot(rank + step, slot))
        for rank in range(RANKS)
        if 0 <= rank + step < RANKS
        for slot in range(COLS // PART)
    ]


def group_list():
    return [
        [PLANE_OF[band] * 8 + slot_of(band, turn) for turn in range(LEVELS)] for band in range(PLANES)
    ]


def left_lanes(shape):
    return lax.broadcasted_iota(jnp.int32, shape, len(shape) - 1) < ORDER


def call(kernel, outs, operands, scratch=(), scalars=0):
    return pl.pallas_call(
        kernel,
        out_shape=[jax.ShapeDtypeStruct(shape, dtype) for shape, dtype in outs],
        in_specs=[
            pl.BlockSpec(memory_space=pltpu.SMEM if n < scalars else VMEM) for n in range(len(operands))
        ],
        out_specs=[pl.BlockSpec(memory_space=VMEM) for _ in outs],
        scratch_shapes=list(scratch),
        compiler_params=pltpu.CompilerParams(vmem_limit_bytes=16 * 1024 * 1024),
    )(*operands)


def put_block(ref, row, values):
    for part in range(LINKS):
        start = part * BLOCK + row
        ref[start : start + values.shape[0], :] = values[:, part * 128 : (part + 1) * 128]


def prepare_kernel(shift_ref, pattern_ref, rhs_ref, factor_ref, diag_ref, out_ref):
    lane = lax.broadcasted_iota(jnp.int32, (16, WIDE), 1)
    entries = jnp.zeros((16, WIDE), jnp.int32)
    for n in range(SLOTS):
        for m in range(LINKS):
            entry = jnp.clip(pattern_ref[n, m], 0, WINDOW - 1)
            entries = jnp.where(lane == LINKS * n + m, entry, entries)
    entries = entries.astype(F32).astype(BF16)
    for i in range(PAIRS):
        couplings, sides = [], []
        for n in (i, i + PAIRS):
            diag = diag_ref[n]
            factor = jnp.concatenate([factor_ref[n, m] for m in range(LINKS)], axis=1)
            couplings.append(jnp.dot(diag, factor, preferred_element_type=F32))
            sides.append(jnp.dot(diag, rhs_ref[n], preferred_element_type=F32))
        both = jnp.concatenate(couplings, axis=1).astype(BF16)
        put_block(out_ref, i * ORDER, both)
        turned = jnp.concatenate(sides, axis=0).T.astype(BF16)
        for j in range(COLS // PART):
            row = SHARD + turn_of_slot(j, shift_ref[0]) * PIECE + i * PART
            out_ref[pl.ds(pl.multiple_of(row, 16), PART), :] = turned[j * PART : (j + 1) * PART, :]
    put_block(out_ref, ROWS, entries)


def finish_kernel(shift_ref, parts_ref, diag_ref, forward_ref, backward_ref):
    for i in range(PAIRS):
        for kind in range(2):
            columns = jnp.concatenate(
                [parts_ref[turn_of_slot(j, shift_ref[0]), kind, i] for j in range(COLS // PART)], axis=0
            )
            turned = columns.astype(F32).T.astype(BF16)
            for n, rows in ((i, turned[:ORDER]), (i + PAIRS, turned[ORDER:])):
                if kind == 0:
                    forward_ref[n] = rows
                else:
                    backward_ref[n] = lax.dot_general(
                        diag_ref[n], rows, (((0,), (0,)), ((), ())), preferred_element_type=F32
                    ).astype(BF16)


def put_window(window_ref, source_ref, base):
    for i in range(PAIRS):
        pair = source_ref[i].astype(F32)
        swapped = pltpu.roll(pair, ORDER, 1)
        left = left_lanes(pair.shape)
        window_ref[base + i] = jnp.where(left, pair, swapped).astype(BF16)
        window_ref[base + PAIRS + i] = jnp.where(left, swapped, pair).astype(BF16)


def level_weights(level, state_ref, own_ref, other_ref):
    mine = state_ref[1] == level // 4
    index = shard_index(state_ref, level)

    def weights(i):
        parts = []
        for part in range(LINKS):
            rows = pl.ds(part * BLOCK + i * ORDER, ORDER)
            parts.append(jnp.where(mine, own_ref[index, rows, :], other_ref[index, rows, :]))
        return jnp.concatenate(parts, axis=1)

    return weights


def shard_index(state_ref, level):
    return (state_ref[0] + LEVELS - level) & 3


def forward_pair(pattern_ref, level, index, weights, window_ref, rhs_ref, i):
    w = weights(i)
    sums = []
    for n in (i, i + PAIRS):
        a, b, c = (window_ref[pattern_ref[index, LINKS * n + m]] for m in range(LINKS))
        left = left_lanes(a.shape)
        zero = jnp.zeros_like(a)
        if n < PAIRS:
            picked, lanes = (jnp.where(left, a, b), jnp.where(left, c, zero)), slice(0, 256)
        else:
            picked, lanes = (jnp.where(left, zero, a), jnp.where(left, b, c)), slice(128, 384)
        sums.append(
            lax.dot_general(
                jnp.concatenate(picked, axis=1),
                w[:, lanes],
                (((1,), (1,)), ((), ())),
                preferred_element_type=F32,
            )
        )
    return (rhs_ref[level, i].astype(F32) - jnp.concatenate(sums, axis=1)).astype(BF16)


def fill_window(window_ref, own_ref, below_ref, above_ref):
    put_window(window_ref, below_ref, 0)
    put_window(window_ref, own_ref, SLOTS)
    put_window(window_ref, above_ref, 2 * SLOTS)


def level_kernel(level, step, state_ref, pattern_ref, own_ref, other_ref, *refs):
    weights = level_weights(level, state_ref, own_ref, other_ref)
    index = shard_index(state_ref, level) + 4 * (state_ref[1] != level // 4).astype(jnp.int32)
    step(pattern_ref, level, index, weights, *refs)


def forward_step(
    pattern_ref, level, index, weights, rhs_ref, own_ref, below_ref, above_ref, out_ref, window_ref
):
    fill_window(window_ref, own_ref, below_ref, above_ref)
    for i in range(PAIRS):
        out_ref[i] = forward_pair(pattern_ref, level, index, weights, window_ref, rhs_ref, i)


def spread(pattern_ref, index, weights, reduced, sums_ref, total_ref):
    for q in range(WINDOW):
        total_ref[q] = jnp.zeros(total_ref.shape[1:], F32)
    for i in range(PAIRS):
        pair = reduced[i].astype(F32)
        rows = jnp.concatenate([pair, pltpu.roll(pair, ORDER, 1)], axis=0)[:, :ORDER].astype(BF16)
        products = jnp.dot(rows, weights(i), preferred_element_type=F32)
        for n, product in ((i, products[:PART, :256]), (i + PAIRS, products[PART:, 128:])):
            head, tail = product[:, :128], product[:, 128:]
            left = left_lanes(head.shape)
            zero = jnp.zeros_like(head)
            if n < PAIRS:
                terms = (jnp.where(left, head, zero), jnp.where(left, zero, head), jnp.where(left, tail, zero))
            else:
                terms = (jnp.where(left, zero, head), jnp.where(left, tail, zero), jnp.where(left, zero, tail))
            for m in range(LINKS):
                total_ref[pattern_ref[index, LINKS * n + m]] += terms[m]
    for part in range(LINKS):
        for i in range(PAIRS):
            one = total_ref[part * SLOTS + i]
            two = total_ref[part * SLOTS + PAIRS + i]
            left = left_lanes(one.shape)
            one = one + pltpu.roll(one, ORDER, 1)
            two = two + pltpu.roll(two, ORDER, 1)
            sums_ref[part, i] = jnp.where(left, one, two).astype(BF16)


def turn_step(
    pattern_ref, level, index, weights, rhs_ref, own_ref, below_ref, above_ref,
    out_ref, sums_ref, window_ref, total_ref,
):
    fill_window(window_ref, own_ref, below_ref, above_ref)
    solved = []
    for i in range(PAIRS):
        solved.append(forward_pair(pattern_ref, level, index, weights, window_ref, rhs_ref, i))
        out_ref[i] = solved[i]
    spread(pattern_ref, index, weights, solved, sums_ref, total_ref)


def reduce(forward_ref, own_ref, below_ref, above_ref, out_ref):
    reduced = []
    for i in range(PAIRS):
        incoming = own_ref[1, i].astype(F32) + below_ref[i].astype(F32) + above_ref[i].astype(F32)
        reduced.append((forward_ref[i].astype(F32) - incoming).astype(BF16))
        out_ref[i] = reduced[i]
    return reduced


def backward_step(
    pattern_ref, level, index, weights, forward_ref, own_ref, below_ref, above_ref, out_ref, sums_ref, total_ref
):
    reduced = reduce(forward_ref, own_ref, below_ref, above_ref, out_ref)
    spread(pattern_ref, index, weights, reduced, sums_ref, total_ref)


def last_kernel(sums_ref, below_ref, above_ref, *refs):
    forward, reduced, packed_ref = refs[:LEVELS], refs[LEVELS:-1], refs[-1]
    for level in range(LEVELS):
        packed_ref[level, 0] = forward[level][...]
        if level > 0:
            packed_ref[level, 1] = reduced[level - 1][...]
    reduce(forward[0], sums_ref, below_ref, above_ref, packed_ref.at[0, 1])


def per_device(right_side, factor_blocks, diag_inverse, pattern):
    up, down = neighbour_pairs(1), neighbour_pairs(-1)
    to_group = level_pairs()
    to_native = [(b, a) for a, b in to_group]
    groups = group_list()
    solved_shape = ((PAIRS, PART, 128), BF16)
    sums_shape = ((LINKS, PAIRS, PART, 128), BF16)
    window = VMEM((WINDOW, PART, 128), BF16)
    total = VMEM((WINDOW, PART, 128), F32)

    def exchange(to_above, to_below):
        return lax.ppermute(to_above, AXES, up), lax.ppermute(to_below, AXES, down)

    lvl = lax.axis_index("lvl")
    plane, x, core = lvl // 8, lvl % 8 // 2, lvl % 2
    band = (plane - PLANE_OF[0]) % PLANES
    state = jnp.stack([(x + band) % 4, core]).astype(jnp.int32)
    shift = ((x * 2 + core) % 4).astype(jnp.int32).reshape(1)

    (prepared,) = call(
        prepare_kernel,
        [((SHARD + COLS // PART * PIECE, 128), BF16)],
        (shift, pattern, right_side, factor_blocks, diag_inverse),
        scalars=2,
    )
    prepared = lax.ppermute(prepared, AXES, to_group)
    weights, rhs = prepared[:SHARD], prepared[SHARD:].reshape(LEVELS, PAIRS, PART, 128)

    def along_x(steps):
        pairs = [(i, i // 8 * 8 + (i % 8 + 2 * steps) % 8) for i in range(128)]
        return lax.ppermute(weights, "lvl", pairs)

    gathered = (along_x(1), along_x(2), along_x(3))
    rhs = lax.all_to_all(rhs, "lvl", 0, 0, axis_index_groups=groups)
    latest = rhs[0]
    near = exchange(latest, latest)
    *gathered, below, above = lax.optimization_barrier((*gathered, *near))
    near = (below, above)
    own = jnp.stack([weights, *gathered])
    other = lax.ppermute(own, "lvl", [(i, i ^ 1) for i in range(128)])
    patterns = jnp.concatenate([own[:, ROWS, :WINDOW], other[:, ROWS, :WINDOW]]).astype(jnp.int32)

    def level_call(level, step, arrays, outs, scratch):
        kernel = functools.partial(level_kernel, level, step)
        return call(kernel, outs, (state, patterns, own, other) + arrays, scratch, scalars=2)

    forward = [latest]
    for level in range(1, LEVELS):
        below, above = near if level == 1 else exchange(latest, latest)
        last = level == LEVELS - 1
        latest, *rest = level_call(
            level,
            turn_step if last else forward_step,
            (rhs, latest, below, above),
            [solved_shape, sums_shape] if last else [solved_shape],
            [window, total] if last else [window],
        )
        forward.append(latest)
    (sums,) = rest

    reduced = [latest]
    for level in range(LEVELS - 2, 0, -1):
        below, above = exchange(sums[2], sums[0])
        latest, sums = level_call(
            level,
            backward_step,
            (forward[level], sums, below, above),
            [solved_shape, sums_shape],
            [total],
        )
        reduced.append(latest)
    below, above = exchange(sums[2], sums[0])
    (packed,) = call(
        last_kernel,
        [((LEVELS, 2, PAIRS, PART, 128), BF16)],
        (sums, below, above, *forward, *reduced[::-1]),
    )

    parts = lax.all_to_all(packed, "lvl", 0, 0, axis_index_groups=groups)
    parts = lax.ppermute(parts, AXES, to_native)
    out_shape = ((SLOTS, ORDER, COLS), BF16)
    return call(finish_kernel, [out_shape] * 2, (shift, parts, diag_inverse), scalars=1)


def solution(mesh):
    return jax.shard_map(
        per_device,
        mesh=mesh,
        in_specs=(
            P(AXES, None, None),
            P(AXES, None, None, None),
            P(AXES, None, None),
            P(AXES, None),
        ),
        out_specs=(P(AXES, None, None), P(AXES, None, None)),
        check_vma=False,
    )
```

```python
import functools

import jax
import jax.numpy as jnp
from jax import lax
from jax.experimental import pallas as pl
from jax.experimental.pallas import tpu as pltpu
from jax.sharding import PartitionSpec as P

LEVELS = 8
RANKS = 64
SLOTS = 14
PAIRS = 7
LINKS = 3
ORDER = 64
COLS = 128
PART = 16
BOTH = 2 * PART
WINDOW = LINKS * SLOTS
ROTATION = 96
PLANES = 16
ROWS = PAIRS * ORDER
BLOCK = ROWS + 16
SHARD = LINKS * BLOCK
PIECE = PAIRS * 16
WIDE = 2 * LINKS * ORDER
CHUNK = LEVELS // 2
AXES = ("lvl", "row")
BF16 = jnp.bfloat16
F32 = jnp.float32
VMEM = pltpu.VMEM

PLANE_OF = [(band + 14) % PLANES for band in range(PLANES)]


def slot_of(band, turn):
    return (turn - band) % 4 * 2 + 1 - turn // 4


def turn_of_slot(slot, shift):
    return (slot // 2 + shift) % 4 + (1 - slot % 2) * 4


def place_slot(rank, slot):
    band, side = divmod(rank, 4)
    y = side if band % 2 == 0 else 3 - side
    return (PLANE_OF[band] * 8 + slot) * 4 + y


def place(rank, turn):
    return place_slot(rank, slot_of(rank // 4, turn))


def native(level, rank):
    return (level * RANKS + rank - ROTATION) % (LEVELS * RANKS)


def level_pairs(first=0):
    return [
        (native(level, rank), place(rank, level))
        for level in range(first, LEVELS)
        for rank in range(RANKS)
    ]


def neighbour_pairs(step):
    return [
        (place_slot(rank, slot), place_slot(rank + step, slot))
        for rank in range(RANKS)
        if 0 <= rank + step < RANKS
        for slot in range(1, COLS // PART, 2)
    ]


def group_list():
    return [
        [PLANE_OF[band] * 8 + slot_of(band, turn) for turn in range(LEVELS)] for band in range(PLANES)
    ]


def left_lanes(shape):
    return lax.broadcasted_iota(jnp.int32, shape, len(shape) - 1) < ORDER


def call(kernel, outs, operands, scratch=(), scalars=0, cost=None):
    return pl.pallas_call(
        kernel,
        out_shape=[jax.ShapeDtypeStruct(shape, dtype) for shape, dtype in outs],
        in_specs=[
            pl.BlockSpec(memory_space=pltpu.SMEM if n < scalars else VMEM) for n in range(len(operands))
        ],
        out_specs=[pl.BlockSpec(memory_space=VMEM) for _ in outs],
        scratch_shapes=list(scratch),
        compiler_params=pltpu.CompilerParams(vmem_limit_bytes=16 * 1024 * 1024),
        cost_estimate=cost,
    )(*operands)


def put_block(ref, row, values):
    for part in range(LINKS):
        start = part * BLOCK + row
        ref[start : start + values.shape[0], :] = values[:, part * 128 : (part + 1) * 128]


def prepare_kernel(
    shift_ref, pattern_ref, rhs_hbm, factor_hbm, diag_hbm, out_ref, rhs_t_ref, rhs_ref, factor_ref, diag_ref, sems
):
    arrays = ((diag_hbm, diag_ref), (rhs_hbm, rhs_ref), (factor_hbm, factor_ref))
    copies = []
    for half in range(2):
        rows = pl.ds(half * PAIRS, PAIRS)
        for n, (source, target) in enumerate(arrays):
            copies.append(pltpu.make_async_copy(source.at[rows], target.at[rows], sems.at[half * 3 + n]))
    for copy in copies:
        copy.start()
    lane = lax.broadcasted_iota(jnp.int32, (16, WIDE), 1)
    entries = jnp.zeros((16, WIDE), jnp.int32)
    for n in range(SLOTS):
        for m in range(LINKS):
            entry = jnp.clip(pattern_ref[m, n], 0, WINDOW - 1)
            entries = jnp.where(lane == LINKS * n + m, entry, entries)
    entries = entries.astype(F32).astype(BF16)
    for copy in copies:
        copy.wait()
    for i in range(PAIRS):
        couplings, sides = [], []
        for n in (i, i + PAIRS):
            diag = diag_ref[n]
            factor = jnp.concatenate([factor_ref[n, m] for m in range(LINKS)], axis=1)
            couplings.append(jnp.dot(diag, factor, preferred_element_type=F32))
            sides.append(jnp.dot(diag, rhs_ref[n], preferred_element_type=F32))
        both = jnp.concatenate(couplings, axis=1).astype(BF16)
        put_block(out_ref, i * ORDER, both)
        turned = jnp.concatenate(sides, axis=0).T.astype(BF16)
        for j in range(COLS // PART):
            rhs_t_ref[turn_of_slot(j, shift_ref[0]), i] = turned[j * PART : (j + 1) * PART, :]
    put_block(out_ref, ROWS, entries)


def finish_kernel(shift_ref, parts_ref, diag_ref, forward_ref, backward_ref):
    for i in range(PAIRS):
        for kind in range(2):
            columns = jnp.concatenate(
                [parts_ref[turn_of_slot(j, shift_ref[0]), kind, i] for j in range(COLS // PART)], axis=0
            )
            turned = columns.astype(F32).T.astype(BF16)
            for n, rows in ((i, turned[:ORDER]), (i + PAIRS, turned[ORDER:])):
                if kind == 0:
                    forward_ref[n] = rows
                else:
                    backward_ref[n] = lax.dot_general(
                        diag_ref[n], rows, (((0,), (0,)), ((), ())), preferred_element_type=F32
                    ).astype(BF16)


def copy_kernel(source_ref, out_ref):
    out_ref[...] = source_ref[...]


def put_window(window_ref, source_ref, base):
    for i in range(PAIRS):
        pair = source_ref[i].astype(F32)
        swapped = pltpu.roll(pair, ORDER, 1)
        left = left_lanes(pair.shape)
        window_ref[base + i] = jnp.where(left, pair, swapped).astype(BF16)
        window_ref[base + PAIRS + i] = jnp.where(left, swapped, pair).astype(BF16)


def level_weights(index, shards_ref):
    def weights(i):
        return jnp.concatenate(
            [shards_ref[index, pl.ds(part * BLOCK + i * ORDER, ORDER), :] for part in range(LINKS)], axis=1
        )

    return weights


def forward_pair(pattern, level, weights, window_ref, rhs_ref, i):
    w = weights(i)
    sums = []
    for n in (i, i + PAIRS):
        a, b, c = (window_ref[pattern(n, m)] for m in range(LINKS))
        left = left_lanes(a.shape)
        zero = jnp.zeros_like(a)
        if n < PAIRS:
            picked, lanes = (jnp.where(left, a, b), jnp.where(left, c, zero)), slice(0, 256)
        else:
            picked, lanes = (jnp.where(left, zero, a), jnp.where(left, b, c)), slice(128, 384)
        sums.append(
            lax.dot_general(
                jnp.concatenate(picked, axis=1),
                w[:, lanes],
                (((1,), (1,)), ((), ())),
                preferred_element_type=F32,
            )
        )
    return (rhs_ref[level, i].astype(F32) - jnp.concatenate(sums, axis=1)).astype(BF16)


def fill_window(window_ref, own_ref, below_ref, above_ref):
    put_window(window_ref, below_ref, 0)
    put_window(window_ref, own_ref, SLOTS)
    put_window(window_ref, above_ref, 2 * SLOTS)


def level_kernel(level, step, table_ref, shards_ref, *refs):
    index = (table_ref[0, 0] + LEVELS - level) & 3
    row = table_ref[pl.ds(index, 1), :]
    step(lambda n, m: row[0, 1 + LINKS * n + m], level, level_weights(index, shards_ref), *refs)


def forward_step(
    pattern, level, weights, rhs_ref, own_ref, below_ref, above_ref, out_ref, window_ref
):
    fill_window(window_ref, own_ref, below_ref, above_ref)
    for i in range(PAIRS):
        out_ref[i] = forward_pair(pattern, level, weights, window_ref, rhs_ref, i)


def spread(pattern, weights, reduced, sums_ref, total_ref):
    for q in range(WINDOW):
        total_ref[q] = jnp.zeros(total_ref.shape[1:], F32)
    for i in range(PAIRS):
        pair = reduced[i].astype(F32)
        rows = jnp.concatenate([pair, pltpu.roll(pair, ORDER, 1)], axis=0)[:, :ORDER].astype(BF16)
        products = jnp.dot(rows, weights(i), preferred_element_type=F32)
        for n, product in ((i, products[:BOTH, :256]), (i + PAIRS, products[BOTH:, 128:])):
            head, tail = product[:, :128], product[:, 128:]
            left = left_lanes(head.shape)
            zero = jnp.zeros_like(head)
            if n < PAIRS:
                terms = (jnp.where(left, head, zero), jnp.where(left, zero, head), jnp.where(left, tail, zero))
            else:
                terms = (jnp.where(left, zero, head), jnp.where(left, tail, zero), jnp.where(left, zero, tail))
            for m in range(LINKS):
                total_ref[pattern(n, m)] += terms[m]
    for part in range(LINKS):
        for i in range(PAIRS):
            one = total_ref[part * SLOTS + i]
            two = total_ref[part * SLOTS + PAIRS + i]
            left = left_lanes(one.shape)
            one = one + pltpu.roll(one, ORDER, 1)
            two = two + pltpu.roll(two, ORDER, 1)
            sums_ref[part, i] = jnp.where(left, one, two).astype(BF16)


def turn_step(
    pattern, level, weights, rhs_ref, own_ref, below_ref, above_ref,
    out_ref, sums_ref, window_ref, total_ref,
):
    fill_window(window_ref, own_ref, below_ref, above_ref)
    solved = []
    for i in range(PAIRS):
        solved.append(forward_pair(pattern, level, weights, window_ref, rhs_ref, i))
        out_ref[i] = solved[i]
    spread(pattern, weights, solved, sums_ref, total_ref)


def reduce(forward_ref, own_ref, below_ref, above_ref, out_ref):
    reduced = []
    for i in range(PAIRS):
        incoming = own_ref[1, i].astype(F32) + below_ref[i].astype(F32) + above_ref[i].astype(F32)
        reduced.append((forward_ref[i].astype(F32) - incoming).astype(BF16))
        out_ref[i] = reduced[i]
    return reduced


def backward_step(
    pattern, level, weights, forward_ref, own_ref, below_ref, above_ref, out_ref, sums_ref, total_ref
):
    reduced = reduce(forward_ref, own_ref, below_ref, above_ref, out_ref)
    spread(pattern, weights, reduced, sums_ref, total_ref)


def last_kernel(sums_ref, below_ref, above_ref, *refs):
    forward, reduced, last_ref = refs[:LEVELS], refs[LEVELS:-3], refs[-1]
    reduce(forward[0], sums_ref, below_ref, above_ref, last_ref)
    for core in range(2):
        columns = pl.ds(core * PART, PART)
        for level in range(LEVELS):
            refs[core - 3][level, 0] = forward[level][:, columns, :]
            back_ref = reduced[level - 1] if level else last_ref
            refs[core - 3][level, 1] = back_ref[:, columns, :]


def per_device(right_side, factor_blocks, diag_inverse, pattern):
    up, down = neighbour_pairs(1), neighbour_pairs(-1)
    to_group = level_pairs()
    to_native = [(b, a) for a, b in to_group]
    groups = group_list()
    solved_shape = ((PAIRS, BOTH, 128), BF16)
    sums_shape = ((LINKS, PAIRS, BOTH, 128), BF16)
    window = VMEM((WINDOW, BOTH, 128), BF16)
    total = VMEM((WINDOW, BOTH, 128), F32)

    def exchange(to_above, to_below):
        return lax.ppermute(to_above, AXES, up), lax.ppermute(to_below, AXES, down)

    lvl = lax.axis_index("lvl")
    plane, x, core = lvl // 8, lvl % 8 // 2, lvl % 2
    band = (plane - PLANE_OF[0]) % PLANES
    state = ((x + band) % 4).astype(jnp.int32).reshape(1)
    shift = ((x * 2 + core) % 4).astype(jnp.int32).reshape(1)

    stored = (right_side, factor_blocks, diag_inverse)
    weights, rhs = pl.pallas_call(
        prepare_kernel,
        out_shape=[
            jax.ShapeDtypeStruct((SHARD, 128), BF16),
            jax.ShapeDtypeStruct((LEVELS, PAIRS, PART, 128), BF16),
        ],
        in_specs=[pl.BlockSpec(memory_space=pltpu.SMEM)] * 2 + [pl.BlockSpec(memory_space=pltpu.HBM)] * 3,
        out_specs=[pl.BlockSpec(memory_space=VMEM)] * 2,
        scratch_shapes=[VMEM(array.shape, BF16) for array in stored] + [pltpu.SemaphoreType.DMA((6,))],
        compiler_params=pltpu.CompilerParams(vmem_limit_bytes=16 * 1024 * 1024),
    )(shift, pattern.T, *stored)
    rhs = lax.ppermute(rhs, AXES, to_group)
    weights = lax.ppermute(weights, AXES, level_pairs(1))
    cost = pl.CostEstimate(flops=50 * 10**9, bytes_accessed=SHARD * 512, transcendentals=0)
    (weights,) = call(copy_kernel, [((SHARD, 128), BF16)], (weights,), cost=cost)

    def along_x(value, core):
        def moved(steps):
            pairs = [(i, i // 8 * 8 + (i % 8 + 2 * steps) % 8) for i in range(core, 128, 2)]
            return lax.ppermute(value, "lvl", pairs)

        return moved(1), moved(2), moved(3)

    to_first = [(i + 1, i) for i in range(0, 128, 2)]
    to_second = [(i, i + 1) for i in range(0, 128, 2)]
    low = along_x(weights, 1)
    rhs = lax.all_to_all(rhs, "lvl", 0, 0, axis_index_groups=groups)
    rhs = jnp.concatenate([lax.ppermute(rhs, "lvl", to_second), rhs], axis=2)
    latest = rhs[0]
    near = exchange(latest, latest)
    *low, below, above = lax.optimization_barrier((*low, *near))
    near = (below, above)
    low = jnp.stack([weights, *low])
    def gather_high(solved):
        ready = lax.ppermute(solved, "lvl", to_first).reshape(PAIRS * BOTH, 128)
        shards = jnp.concatenate([weights, ready])
        return lax.ppermute(jnp.stack([shards, *along_x(shards, 0)]), "lvl", to_second)

    def level_call(level, step, arrays, outs, scratch):
        kernel = functools.partial(level_kernel, level, step)
        shards = high if level >= CHUNK else low
        patterns = shards[:, ROWS, :WINDOW].astype(jnp.int32)
        table = jnp.concatenate([jnp.broadcast_to(state, (4, 1)), patterns], axis=1)
        cost = pl.CostEstimate(flops=20 * 10**9, bytes_accessed=SHARD * 512, transcendentals=0)
        return call(kernel, outs, (table, shards) + arrays, scratch, cost=cost)

    forward = [latest]
    for level in range(1, LEVELS):
        below, above = near if level == 1 else exchange(latest, latest)
        last = level == LEVELS - 1
        latest, *rest = level_call(
            level,
            turn_step if last else forward_step,
            (rhs, latest, below, above),
            [solved_shape, sums_shape] if last else [solved_shape],
            [window, total] if last else [window],
        )
        forward.append(latest)
        if level == 1:
            high = gather_high(latest)
    (sums,) = rest

    reduced = [latest]
    for level in range(LEVELS - 2, 0, -1):
        below, above = exchange(sums[2], sums[0])
        latest, sums = level_call(
            level,
            backward_step,
            (forward[level], sums, below, above),
            [solved_shape, sums_shape],
            [total],
        )
        reduced.append(latest)
    below, above = exchange(sums[2], sums[0])
    packed_shape = ((LEVELS, 2, PAIRS, PART, 128), BF16)
    for_first, for_second = call(
        last_kernel, [packed_shape] * 2, (sums, below, above, *forward, *reduced[::-1]), [VMEM(*solved_shape)]
    )
    packed = jnp.where(core == 1, for_second, lax.ppermute(for_first, "lvl", to_first))

    parts = lax.all_to_all(packed, "lvl", 0, 0, axis_index_groups=groups)
    parts = lax.ppermute(parts, AXES, to_native)
    out_shape = ((SLOTS, ORDER, COLS), BF16)
    return call(finish_kernel, [out_shape] * 2, (shift, parts, diag_inverse), scalars=1)


def solution(mesh):
    return jax.shard_map(
        per_device,
        mesh=mesh,
        in_specs=(
            P(AXES, None, None),
            P(AXES, None, None, None),
            P(AXES, None, None),
            P(AXES, None),
        ),
        out_specs=(P(AXES, None, None), P(AXES, None, None)),
        check_vma=False,
    )
```

```python
import functools

import jax
import jax.numpy as jnp
from jax import lax
from jax.experimental import pallas as pl
from jax.experimental.pallas import tpu as pltpu
from jax.sharding import PartitionSpec as P

LEVELS = 8
RANKS = 64
SLOTS = 14
PAIRS = 7
LINKS = 3
ORDER = 64
COLS = 128
PART = 16
BOTH = 2 * PART
WINDOW = LINKS * SLOTS
ROTATION = 96
PLANES = 16
ROWS = PAIRS * ORDER
BLOCK = ROWS + 16
SHARD = LINKS * BLOCK
PIECE = PAIRS * 16
WIDE = 2 * LINKS * ORDER
CHUNK = LEVELS // 2
AXES = ("lvl", "row")
BF16 = jnp.bfloat16
F32 = jnp.float32
VMEM = pltpu.VMEM

PLANE_OF = [(band + 14) % PLANES for band in range(PLANES)]


def slot_of(band, turn):
    return (turn - band) % 4 * 2 + 1 - turn // 4


def turn_of_slot(slot, shift):
    return (slot // 2 + shift) % 4 + (1 - slot % 2) * 4


def place_slot(rank, slot):
    band, side = divmod(rank, 4)
    y = side if band % 2 == 0 else 3 - side
    return (PLANE_OF[band] * 8 + slot) * 4 + y


def place(rank, turn):
    return place_slot(rank, slot_of(rank // 4, turn))


def native(level, rank):
    return (level * RANKS + rank - ROTATION) % (LEVELS * RANKS)


def level_pairs(first=0):
    return [
        (native(level, rank), place(rank, level))
        for level in range(first, LEVELS)
        for rank in range(RANKS)
    ]


def neighbour_pairs(step):
    return [
        (place_slot(rank, slot), place_slot(rank + step, slot))
        for rank in range(RANKS)
        if 0 <= rank + step < RANKS
        for slot in range(1, COLS // PART, 2)
    ]


def group_list():
    return [
        [PLANE_OF[band] * 8 + slot_of(band, turn) for turn in range(LEVELS)] for band in range(PLANES)
    ]


def left_lanes(shape):
    return lax.broadcasted_iota(jnp.int32, shape, len(shape) - 1) < ORDER


def call(kernel, outs, operands, scratch=(), scalars=0, cost=None):
    return pl.pallas_call(
        kernel,
        out_shape=[jax.ShapeDtypeStruct(shape, dtype) for shape, dtype in outs],
        in_specs=[
            pl.BlockSpec(memory_space=pltpu.SMEM if n < scalars else VMEM) for n in range(len(operands))
        ],
        out_specs=[pl.BlockSpec(memory_space=VMEM) for _ in outs],
        scratch_shapes=list(scratch),
        compiler_params=pltpu.CompilerParams(vmem_limit_bytes=16 * 1024 * 1024),
        cost_estimate=cost,
    )(*operands)


def put_block(ref, row, values):
    for part in range(LINKS):
        start = part * BLOCK + row
        ref[start : start + values.shape[0], :] = values[:, part * 128 : (part + 1) * 128]


def prepare_rhs_kernel(shift_ref, rhs_ref, diag_ref, out_ref):
    shift = shift_ref[0, 0]
    for i in range(PAIRS):
        sides = [
            jnp.dot(diag_ref[n], rhs_ref[n], preferred_element_type=F32) for n in (i, i + PAIRS)
        ]
        turned = jnp.concatenate(sides, axis=0).T.astype(BF16)
        for j in range(COLS // PART):
            out_ref[turn_of_slot(j, shift), i] = turned[j * PART : (j + 1) * PART, :]


def prepare_weights_kernel(pattern_ref, factor_ref, diag_ref, out_ref):
    patterns = pattern_ref[...]
    lane = lax.broadcasted_iota(jnp.int32, (16, WIDE), 1)
    entries = jnp.zeros((16, WIDE), jnp.int32)
    for n in range(SLOTS):
        for m in range(LINKS):
            entry = jnp.clip(patterns[m, n], 0, WINDOW - 1)
            entries = jnp.where(lane == LINKS * n + m, entry, entries)
    put_block(out_ref, ROWS, entries.astype(F32).astype(BF16))
    for i in range(PAIRS):
        couplings = []
        for n in (i, i + PAIRS):
            factor = jnp.concatenate([factor_ref[n, m] for m in range(LINKS)], axis=1)
            couplings.append(jnp.dot(diag_ref[n], factor, preferred_element_type=F32))
        put_block(out_ref, i * ORDER, jnp.concatenate(couplings, axis=1).astype(BF16))


def finish_kernel(shift_ref, parts_ref, diag_ref, forward_ref, backward_ref):
    for i in range(PAIRS):
        for kind in range(2):
            columns = jnp.concatenate(
                [parts_ref[turn_of_slot(j, shift_ref[0, 0]), kind, i] for j in range(COLS // PART)], axis=0
            )
            turned = columns.astype(F32).T.astype(BF16)
            for n, rows in ((i, turned[:ORDER]), (i + PAIRS, turned[ORDER:])):
                if kind == 0:
                    forward_ref[n] = rows
                else:
                    backward_ref[n] = lax.dot_general(
                        diag_ref[n], rows, (((0,), (0,)), ((), ())), preferred_element_type=F32
                    ).astype(BF16)


def copy_kernel(source_ref, out_ref):
    out_ref[...] = source_ref[...]


def put_window(window_ref, source_ref, base):
    for i in range(PAIRS):
        pair = source_ref[i].astype(F32)
        swapped = pltpu.roll(pair, ORDER, 1)
        left = left_lanes(pair.shape)
        window_ref[base + i] = jnp.where(left, pair, swapped).astype(BF16)
        window_ref[base + PAIRS + i] = jnp.where(left, swapped, pair).astype(BF16)


def level_weights(index, shards_ref):
    def weights(i):
        return jnp.concatenate(
            [shards_ref[index, pl.ds(part * BLOCK + i * ORDER, ORDER), :] for part in range(LINKS)], axis=1
        )

    return weights


def forward_pair(pattern, level, weights, window_ref, rhs_ref, i):
    w = weights(i)
    sums = []
    for n in (i, i + PAIRS):
        a, b, c = (window_ref[pattern(n, m)] for m in range(LINKS))
        left = left_lanes(a.shape)
        zero = jnp.zeros_like(a)
        if n < PAIRS:
            picked, lanes = (jnp.where(left, a, b), jnp.where(left, c, zero)), slice(0, 256)
        else:
            picked, lanes = (jnp.where(left, zero, a), jnp.where(left, b, c)), slice(128, 384)
        sums.append(
            lax.dot_general(
                jnp.concatenate(picked, axis=1),
                w[:, lanes],
                (((1,), (1,)), ((), ())),
                preferred_element_type=F32,
            )
        )
    return (rhs_ref[level, i].astype(F32) - jnp.concatenate(sums, axis=1)).astype(BF16)


def fill_window(window_ref, own_ref, below_ref, above_ref):
    put_window(window_ref, below_ref, 0)
    put_window(window_ref, own_ref, SLOTS)
    put_window(window_ref, above_ref, 2 * SLOTS)


def level_kernel(level, step, table_ref, shards_ref, *refs):
    index = (table_ref[0, 0] + LEVELS - level) & 3
    row = table_ref[pl.ds(index, 1), :]
    step(lambda n, m: row[0, 1 + LINKS * n + m], level, level_weights(index, shards_ref), *refs)


def forward_step(
    pattern, level, weights, rhs_ref, own_ref, below_ref, above_ref, out_ref, window_ref
):
    fill_window(window_ref, own_ref, below_ref, above_ref)
    for i in range(PAIRS):
        out_ref[i] = forward_pair(pattern, level, weights, window_ref, rhs_ref, i)


def spread(pattern, weights, reduced, sums_ref, total_ref):
    for q in range(WINDOW):
        total_ref[q] = jnp.zeros(total_ref.shape[1:], F32)
    for i in range(PAIRS):
        pair = reduced[i].astype(F32)
        rows = jnp.concatenate([pair, pltpu.roll(pair, ORDER, 1)], axis=0)[:, :ORDER].astype(BF16)
        products = jnp.dot(rows, weights(i), preferred_element_type=F32)
        for n, product in ((i, products[:BOTH, :256]), (i + PAIRS, products[BOTH:, 128:])):
            head, tail = product[:, :128], product[:, 128:]
            left = left_lanes(head.shape)
            zero = jnp.zeros_like(head)
            if n < PAIRS:
                terms = (jnp.where(left, head, zero), jnp.where(left, zero, head), jnp.where(left, tail, zero))
            else:
                terms = (jnp.where(left, zero, head), jnp.where(left, tail, zero), jnp.where(left, zero, tail))
            for m in range(LINKS):
                total_ref[pattern(n, m)] += terms[m]
    for part in range(LINKS):
        for i in range(PAIRS):
            one = total_ref[part * SLOTS + i]
            two = total_ref[part * SLOTS + PAIRS + i]
            left = left_lanes(one.shape)
            one = one + pltpu.roll(one, ORDER, 1)
            two = two + pltpu.roll(two, ORDER, 1)
            sums_ref[part, i] = jnp.where(left, one, two).astype(BF16)


def turn_step(
    pattern, level, weights, rhs_ref, own_ref, below_ref, above_ref,
    out_ref, sums_ref, window_ref, total_ref,
):
    fill_window(window_ref, own_ref, below_ref, above_ref)
    solved = []
    for i in range(PAIRS):
        solved.append(forward_pair(pattern, level, weights, window_ref, rhs_ref, i))
        out_ref[i] = solved[i]
    spread(pattern, weights, solved, sums_ref, total_ref)


def reduce(forward_ref, own_ref, below_ref, above_ref, out_ref):
    reduced = []
    for i in range(PAIRS):
        incoming = own_ref[1, i].astype(F32) + below_ref[i].astype(F32) + above_ref[i].astype(F32)
        reduced.append((forward_ref[i].astype(F32) - incoming).astype(BF16))
        out_ref[i] = reduced[i]
    return reduced


def backward_step(
    pattern, level, weights, forward_ref, own_ref, below_ref, above_ref, out_ref, sums_ref, total_ref
):
    reduced = reduce(forward_ref, own_ref, below_ref, above_ref, out_ref)
    spread(pattern, weights, reduced, sums_ref, total_ref)


def last_kernel(sums_ref, below_ref, above_ref, *refs):
    forward, reduced, last_ref = refs[:LEVELS], refs[LEVELS:-3], refs[-1]
    reduce(forward[0], sums_ref, below_ref, above_ref, last_ref)
    for core in range(2):
        columns = pl.ds(core * PART, PART)
        for level in range(LEVELS):
            refs[core - 3][level, 0] = forward[level][:, columns, :]
            back_ref = reduced[level - 1] if level else last_ref
            refs[core - 3][level, 1] = back_ref[:, columns, :]


def per_device(right_side, factor_blocks, diag_inverse, pattern):
    up, down = neighbour_pairs(1), neighbour_pairs(-1)
    to_group = level_pairs()
    to_native = [(b, a) for a, b in to_group]
    groups = group_list()
    solved_shape = ((PAIRS, BOTH, 128), BF16)
    sums_shape = ((LINKS, PAIRS, BOTH, 128), BF16)
    window = VMEM((WINDOW, BOTH, 128), BF16)
    total = VMEM((WINDOW, BOTH, 128), F32)

    def exchange(to_above, to_below):
        return lax.ppermute(to_above, AXES, up), lax.ppermute(to_below, AXES, down)

    lvl = lax.axis_index("lvl")
    plane, x, core = lvl // 8, lvl % 8 // 2, lvl % 2
    band = (plane - PLANE_OF[0]) % PLANES
    state = ((x + band) % 4).astype(jnp.int32).reshape(1)
    shift = ((x * 2 + core) % 4).astype(jnp.int32).reshape(1, 1)

    (rhs,) = call(
        prepare_rhs_kernel, [((LEVELS, PAIRS, PART, 128), BF16)], (shift, right_side, diag_inverse)
    )
    (weights,) = call(
        prepare_weights_kernel, [((SHARD, 128), BF16)], (pattern.T, factor_blocks, diag_inverse)
    )
    rhs = lax.ppermute(rhs, AXES, to_group)
    weights = lax.ppermute(weights, AXES, level_pairs(1))
    cost = pl.CostEstimate(flops=50 * 10**9, bytes_accessed=SHARD * 512, transcendentals=0)
    (weights,) = call(copy_kernel, [((SHARD, 128), BF16)], (weights,), cost=cost)

    def along_x(value, core):
        def moved(steps):
            pairs = [(i, i // 8 * 8 + (i % 8 + 2 * steps) % 8) for i in range(core, 128, 2)]
            return lax.ppermute(value, "lvl", pairs)

        return moved(1), moved(2), moved(3)

    to_first = [(i + 1, i) for i in range(0, 128, 2)]
    to_second = [(i, i + 1) for i in range(0, 128, 2)]
    low = along_x(weights, 1)
    rhs = lax.all_to_all(rhs, "lvl", 0, 0, axis_index_groups=groups)
    rhs = jnp.concatenate([lax.ppermute(rhs, "lvl", to_second), rhs], axis=2)
    latest = rhs[0]
    near = exchange(latest, latest)
    *low, below, above = lax.optimization_barrier((*low, *near))
    near = (below, above)
    low = jnp.stack([weights, *low])
    def gather_high(solved):
        ready = lax.ppermute(solved, "lvl", to_first).reshape(PAIRS * BOTH, 128)
        shards = jnp.concatenate([weights, ready])
        return lax.ppermute(jnp.stack([shards, *along_x(shards, 0)]), "lvl", to_second)

    def level_call(level, step, arrays, outs, scratch):
        kernel = functools.partial(level_kernel, level, step)
        shards = high if level >= CHUNK else low
        patterns = shards[:, ROWS, :WINDOW].astype(jnp.int32)
        table = jnp.concatenate([jnp.broadcast_to(state, (4, 1)), patterns], axis=1)
        cost = pl.CostEstimate(flops=20 * 10**9, bytes_accessed=SHARD * 512, transcendentals=0)
        return call(kernel, outs, (table, shards) + arrays, scratch, cost=cost)

    forward = [latest]
    for level in range(1, LEVELS):
        below, above = near if level == 1 else exchange(latest, latest)
        last = level == LEVELS - 1
        latest, *rest = level_call(
            level,
            turn_step if last else forward_step,
            (rhs, latest, below, above),
            [solved_shape, sums_shape] if last else [solved_shape],
            [window, total] if last else [window],
        )
        forward.append(latest)
        if level == 1:
            high = gather_high(latest)
    (sums,) = rest

    reduced = [latest]
    for level in range(LEVELS - 2, 0, -1):
        below, above = exchange(sums[2], sums[0])
        latest, sums = level_call(
            level,
            backward_step,
            (forward[level], sums, below, above),
            [solved_shape, sums_shape],
            [total],
        )
        reduced.append(latest)
    below, above = exchange(sums[2], sums[0])
    packed_shape = ((LEVELS, 2, PAIRS, PART, 128), BF16)
    for_first, for_second = call(
        last_kernel, [packed_shape] * 2, (sums, below, above, *forward, *reduced[::-1]), [VMEM(*solved_shape)]
    )
    packed = jnp.where(core == 1, for_second, lax.ppermute(for_first, "lvl", to_first))

    parts = lax.all_to_all(packed, "lvl", 0, 0, axis_index_groups=groups)
    parts = lax.ppermute(parts, AXES, to_native)
    out_shape = ((SLOTS, ORDER, COLS), BF16)
    return call(finish_kernel, [out_shape] * 2, (shift, parts, diag_inverse))


def solution(mesh):
    return jax.shard_map(
        per_device,
        mesh=mesh,
        in_specs=(
            P(AXES, None, None),
            P(AXES, None, None, None),
            P(AXES, None, None),
            P(AXES, None),
        ),
        out_specs=(P(AXES, None, None), P(AXES, None, None)),
        check_vma=False,
    )
```

```python
import functools

import jax
import jax.numpy as jnp
from jax import lax
from jax.experimental import pallas as pl
from jax.experimental.pallas import tpu as pltpu
from jax.sharding import PartitionSpec as P

LEVELS = 8
RANKS = 64
SLOTS = 14
PAIRS = 7
LINKS = 3
ORDER = 64
COLS = 128
PART = 16
BOTH = 2 * PART
WINDOW = LINKS * SLOTS
ROTATION = 96
PLANES = 16
ROWS = PAIRS * ORDER
BLOCK = ROWS + 16
SHARD = LINKS * BLOCK
PIECE = PAIRS * 16
WIDE = 2 * LINKS * ORDER
CHUNK = LEVELS // 2
AXES = ("lvl", "row")
BF16 = jnp.bfloat16
F32 = jnp.float32
VMEM = pltpu.VMEM

PLANE_OF = [(band + 14) % PLANES for band in range(PLANES)]


def slot_of(band, turn):
    return (turn - band) % 4 * 2 + 1 - turn // 4


def turn_of_slot(slot, shift):
    return (slot // 2 + shift) % 4 + (1 - slot % 2) * 4


def place_slot(rank, slot):
    band, side = divmod(rank, 4)
    y = side if band % 2 == 0 else 3 - side
    return (PLANE_OF[band] * 8 + slot) * 4 + y


def place(rank, turn):
    return place_slot(rank, slot_of(rank // 4, turn))


def native(level, rank):
    return (level * RANKS + rank - ROTATION) % (LEVELS * RANKS)


def level_pairs(first=0):
    return [
        (native(level, rank), place(rank, level))
        for level in range(first, LEVELS)
        for rank in range(RANKS)
    ]


def home_pairs(same):
    pairs = []
    for level in range(LEVELS):
        for rank in range(RANKS):
            band = rank // 4
            if (level // CHUNK == band % 2) == same:
                source = place_slot(rank, (level - band) % 4 * 2)
                pairs.append((source, native(level, rank) - band % 2 * 4))
    return pairs


def neighbour_pairs(step):
    return [
        (place_slot(rank, slot), place_slot(rank + step, slot))
        for rank in range(RANKS)
        if 0 <= rank + step < RANKS
        for slot in range(1, COLS // PART, 2)
    ]


def group_list():
    return [
        [PLANE_OF[band] * 8 + slot_of(band, turn) for turn in range(LEVELS)] for band in range(PLANES)
    ]


def left_lanes(shape):
    return lax.broadcasted_iota(jnp.int32, shape, len(shape) - 1) < ORDER


def call(kernel, outs, operands, scratch=(), scalars=0, cost=None):
    return pl.pallas_call(
        kernel,
        out_shape=[jax.ShapeDtypeStruct(shape, dtype) for shape, dtype in outs],
        in_specs=[
            pl.BlockSpec(memory_space=pltpu.SMEM if n < scalars else VMEM) for n in range(len(operands))
        ],
        out_specs=[pl.BlockSpec(memory_space=VMEM) for _ in outs],
        scratch_shapes=list(scratch),
        compiler_params=pltpu.CompilerParams(vmem_limit_bytes=16 * 1024 * 1024),
        cost_estimate=cost,
    )(*operands)


def put_block(ref, row, values):
    for part in range(LINKS):
        start = part * BLOCK + row
        ref[start : start + values.shape[0], :] = values[:, part * 128 : (part + 1) * 128]


def prepare_rhs_kernel(shift_ref, rhs_ref, diag_ref, out_ref):
    shift = shift_ref[0, 0]
    for i in range(PAIRS):
        sides = [
            jnp.dot(diag_ref[n], rhs_ref[n], preferred_element_type=F32) for n in (i, i + PAIRS)
        ]
        turned = jnp.concatenate(sides, axis=0).T.astype(BF16)
        for j in range(COLS // PART):
            out_ref[turn_of_slot(j, shift), i] = turned[j * PART : (j + 1) * PART, :]


def prepare_weights_kernel(pattern_ref, factor_ref, diag_ref, out_ref):
    patterns = pattern_ref[...]
    lane = lax.broadcasted_iota(jnp.int32, (16, WIDE), 1)
    entries = jnp.zeros((16, WIDE), jnp.int32)
    for n in range(SLOTS):
        for m in range(LINKS):
            entry = jnp.clip(patterns[m, n], 0, WINDOW - 1)
            entries = jnp.where(lane == LINKS * n + m, entry, entries)
    put_block(out_ref, ROWS, entries.astype(F32).astype(BF16))
    for i in range(PAIRS):
        couplings = []
        for n in (i, i + PAIRS):
            factor = jnp.concatenate([factor_ref[n, m] for m in range(LINKS)], axis=1)
            couplings.append(jnp.dot(diag_ref[n], factor, preferred_element_type=F32))
        put_block(out_ref, i * ORDER, jnp.concatenate(couplings, axis=1).astype(BF16))


def finish_forward_kernel(home_ref, parts_ref, out_ref):
    home = home_ref[0, 0]
    for i in range(PAIRS):
        columns = jnp.concatenate([parts_ref[(home + 4 - x) & 3, i] for x in range(4)], axis=0)
        turned = columns.astype(F32).T.astype(BF16)
        out_ref[i] = turned[:ORDER]
        out_ref[i + PAIRS] = turned[ORDER:]


def finish_backward_kernel(shift_ref, parts_ref, diag_ref, out_ref):
    shift = shift_ref[0, 0]
    for i in range(PAIRS):
        columns = jnp.concatenate(
            [parts_ref[turn_of_slot(j, shift), i] for j in range(COLS // PART)], axis=0
        )
        turned = columns.astype(F32).T.astype(BF16)
        for n, reduced in ((i, turned[:ORDER]), (i + PAIRS, turned[ORDER:])):
            out_ref[n] = lax.dot_general(
                diag_ref[n], reduced, (((0,), (0,)), ((), ())), preferred_element_type=F32
            ).astype(BF16)


def pack_kernel(state_ref, *refs):
    for level in range(LEVELS):
        refs[LEVELS][(level + LEVELS - state_ref[0, 0]) & 3, level // CHUNK] = refs[level][...]


def copy_kernel(source_ref, out_ref):
    out_ref[...] = source_ref[...]


def put_window(window_ref, source_ref, base):
    for i in range(PAIRS):
        pair = source_ref[i].astype(F32)
        swapped = pltpu.roll(pair, ORDER, 1)
        left = left_lanes(pair.shape)
        window_ref[base + i] = jnp.where(left, pair, swapped).astype(BF16)
        window_ref[base + PAIRS + i] = jnp.where(left, swapped, pair).astype(BF16)


def level_weights(index, shards_ref):
    def weights(i):
        return jnp.concatenate(
            [shards_ref[index, pl.ds(part * BLOCK + i * ORDER, ORDER), :] for part in range(LINKS)], axis=1
        )

    return weights


def forward_pair(pattern, level, weights, window_ref, rhs_ref, i):
    w = weights(i)
    sums = []
    for n in (i, i + PAIRS):
        a, b, c = (window_ref[pattern(n, m)] for m in range(LINKS))
        left = left_lanes(a.shape)
        zero = jnp.zeros_like(a)
        if n < PAIRS:
            picked, lanes = (jnp.where(left, a, b), jnp.where(left, c, zero)), slice(0, 256)
        else:
            picked, lanes = (jnp.where(left, zero, a), jnp.where(left, b, c)), slice(128, 384)
        sums.append(
            lax.dot_general(
                jnp.concatenate(picked, axis=1),
                w[:, lanes],
                (((1,), (1,)), ((), ())),
                preferred_element_type=F32,
            )
        )
    return (rhs_ref[level, i].astype(F32) - jnp.concatenate(sums, axis=1)).astype(BF16)


def fill_window(window_ref, own_ref, below_ref, above_ref):
    put_window(window_ref, below_ref, 0)
    put_window(window_ref, own_ref, SLOTS)
    put_window(window_ref, above_ref, 2 * SLOTS)


def level_kernel(level, step, table_ref, shards_ref, *refs):
    index = (table_ref[0, 0] + LEVELS - level) & 3
    row = table_ref[pl.ds(index, 1), :]
    step(lambda n, m: row[0, 1 + LINKS * n + m], level, level_weights(index, shards_ref), *refs)


def forward_step(
    pattern, level, weights, rhs_ref, own_ref, below_ref, above_ref, out_ref, window_ref
):
    fill_window(window_ref, own_ref, below_ref, above_ref)
    for i in range(PAIRS):
        out_ref[i] = forward_pair(pattern, level, weights, window_ref, rhs_ref, i)


def spread(pattern, weights, reduced, sums_ref, total_ref):
    for q in range(WINDOW):
        total_ref[q] = jnp.zeros(total_ref.shape[1:], F32)
    for i in range(PAIRS):
        pair = reduced[i].astype(F32)
        rows = jnp.concatenate([pair, pltpu.roll(pair, ORDER, 1)], axis=0)[:, :ORDER].astype(BF16)
        products = jnp.dot(rows, weights(i), preferred_element_type=F32)
        for n, product in ((i, products[:BOTH, :256]), (i + PAIRS, products[BOTH:, 128:])):
            head, tail = product[:, :128], product[:, 128:]
            left = left_lanes(head.shape)
            zero = jnp.zeros_like(head)
            if n < PAIRS:
                terms = (jnp.where(left, head, zero), jnp.where(left, zero, head), jnp.where(left, tail, zero))
            else:
                terms = (jnp.where(left, zero, head), jnp.where(left, tail, zero), jnp.where(left, zero, tail))
            for m in range(LINKS):
                total_ref[pattern(n, m)] += terms[m]
    for part in range(LINKS):
        for i in range(PAIRS):
            one = total_ref[part * SLOTS + i]
            two = total_ref[part * SLOTS + PAIRS + i]
            left = left_lanes(one.shape)
            one = one + pltpu.roll(one, ORDER, 1)
            two = two + pltpu.roll(two, ORDER, 1)
            sums_ref[part, i] = jnp.where(left, one, two).astype(BF16)


def turn_step(
    pattern, level, weights, rhs_ref, own_ref, below_ref, above_ref,
    out_ref, sums_ref, window_ref, total_ref,
):
    fill_window(window_ref, own_ref, below_ref, above_ref)
    solved = []
    for i in range(PAIRS):
        solved.append(forward_pair(pattern, level, weights, window_ref, rhs_ref, i))
        out_ref[i] = solved[i]
    spread(pattern, weights, solved, sums_ref, total_ref)


def reduce(forward_ref, own_ref, below_ref, above_ref, out_ref):
    reduced = []
    for i in range(PAIRS):
        incoming = own_ref[1, i].astype(F32) + below_ref[i].astype(F32) + above_ref[i].astype(F32)
        reduced.append((forward_ref[i].astype(F32) - incoming).astype(BF16))
        out_ref[i] = reduced[i]
    return reduced


def backward_step(
    pattern, level, weights, forward_ref, own_ref, below_ref, above_ref, out_ref, sums_ref, total_ref
):
    reduced = reduce(forward_ref, own_ref, below_ref, above_ref, out_ref)
    spread(pattern, weights, reduced, sums_ref, total_ref)


def last_kernel(forward_ref, sums_ref, below_ref, above_ref, *refs):
    reduced, last_ref = refs[:-3], refs[-1]
    reduce(forward_ref, sums_ref, below_ref, above_ref, last_ref)
    for core in range(2):
        columns = pl.ds(core * PART, PART)
        for level in range(LEVELS):
            back_ref = reduced[level - 1] if level else last_ref
            refs[core - 3][level] = back_ref[:, columns, :]


def per_device(right_side, factor_blocks, diag_inverse, pattern):
    up, down = neighbour_pairs(1), neighbour_pairs(-1)
    to_group = level_pairs()
    to_native = [(b, a) for a, b in to_group]
    groups = group_list()
    solved_shape = ((PAIRS, BOTH, 128), BF16)
    sums_shape = ((LINKS, PAIRS, BOTH, 128), BF16)
    window = VMEM((WINDOW, BOTH, 128), BF16)
    total = VMEM((WINDOW, BOTH, 128), F32)

    def exchange(to_above, to_below):
        return lax.ppermute(to_above, AXES, up), lax.ppermute(to_below, AXES, down)

    lvl = lax.axis_index("lvl")
    plane, x, core = lvl // 8, lvl % 8 // 2, lvl % 2
    band = (plane - PLANE_OF[0]) % PLANES
    state = ((x + band) % 4).astype(jnp.int32).reshape(1)
    shift = ((x * 2 + core) % 4).astype(jnp.int32).reshape(1, 1)

    (rhs,) = call(
        prepare_rhs_kernel, [((LEVELS, PAIRS, PART, 128), BF16)], (shift, right_side, diag_inverse)
    )
    (weights,) = call(
        prepare_weights_kernel, [((SHARD, 128), BF16)], (pattern.T, factor_blocks, diag_inverse)
    )
    rhs = lax.ppermute(rhs, AXES, to_group)
    weights = lax.ppermute(weights, AXES, level_pairs(1))
    cost = pl.CostEstimate(flops=50 * 10**9, bytes_accessed=SHARD * 512, transcendentals=0)
    (weights,) = call(copy_kernel, [((SHARD, 128), BF16)], (weights,), cost=cost)

    def along_x(value, core):
        def moved(steps):
            pairs = [(i, i // 8 * 8 + (i % 8 + 2 * steps) % 8) for i in range(core, 128, 2)]
            return lax.ppermute(value, "lvl", pairs)

        return moved(1), moved(2), moved(3)

    to_first = [(i + 1, i) for i in range(0, 128, 2)]
    to_second = [(i, i + 1) for i in range(0, 128, 2)]
    low = along_x(weights, 1)
    rhs = lax.all_to_all(rhs, "lvl", 0, 0, axis_index_groups=groups)
    rhs = jnp.concatenate([lax.ppermute(rhs, "lvl", to_second), rhs], axis=2)
    latest = rhs[0]
    near = exchange(latest, latest)
    *low, below, above = lax.optimization_barrier((*low, *near))
    near = (below, above)
    low = jnp.stack([weights, *low])
    def gather_high(solved):
        ready = lax.ppermute(solved, "lvl", to_first).reshape(PAIRS * BOTH, 128)
        shards = jnp.concatenate([weights, ready])
        return lax.ppermute(jnp.stack([shards, *along_x(shards, 0)]), "lvl", to_second)

    def level_call(level, step, arrays, outs, scratch):
        kernel = functools.partial(level_kernel, level, step)
        shards = high if level >= CHUNK else low
        patterns = shards[:, ROWS, :WINDOW].astype(jnp.int32)
        table = jnp.concatenate([jnp.broadcast_to(state, (4, 1)), patterns], axis=1)
        cost = pl.CostEstimate(flops=20 * 10**9, bytes_accessed=SHARD * 512, transcendentals=0)
        return call(kernel, outs, (table, shards) + arrays, scratch, cost=cost)

    forward = [latest]
    for level in range(1, LEVELS):
        below, above = near if level == 1 else exchange(latest, latest)
        last = level == LEVELS - 1
        latest, *rest = level_call(
            level,
            turn_step if last else forward_step,
            (rhs, latest, below, above),
            [solved_shape, sums_shape] if last else [solved_shape],
            [window, total] if last else [window],
        )
        forward.append(latest)
        if level == 1:
            high = gather_high(latest)
    (sums,) = rest

    (packed,) = call(pack_kernel, [((4, 2, PAIRS, BOTH, 128), BF16)], (state.reshape(1, 1), *forward))
    packed = lax.ppermute(packed, "lvl", to_first)
    band_odd, stored_low = plane % 2 == 1, (lvl + ROTATION // 4) % 128 // 16 < CHUNK
    stored_level = (lvl + ROTATION // 4) % 128 // 16
    home = ((stored_level + 4 - (x * 2 + core) % 4) % 4).astype(jnp.int32).reshape(1, 1)

    reduced = [latest]
    for level in range(LEVELS - 2, 0, -1):
        below, above = exchange(sums[2], sums[0])
        if level == 5:
            below, above, packed = lax.optimization_barrier((below, above, packed))
            near_parts = [packed[0]]
            for steps in (1, 2, 3):
                pairs = [(i, i // 8 * 8 + (i % 8 + 2 * steps) % 8) for i in range(0, 128, 2)]
                near_parts.append(lax.ppermute(packed[steps], "lvl", pairs))
        if level == 3:
            below, above, *near_parts = lax.optimization_barrier((below, above, *near_parts))
            low_parts = jnp.stack([part[0] for part in near_parts])
            high_parts = jnp.stack([part[1] for part in near_parts])
            same = lax.ppermute(jnp.where(band_odd, high_parts, low_parts), AXES, home_pairs(True))
            swapped = lax.ppermute(jnp.where(band_odd, low_parts, high_parts), AXES, home_pairs(False))
        if level == 1:
            below, above, same, swapped = lax.optimization_barrier((below, above, same, swapped))
        latest, sums = level_call(
            level,
            backward_step,
            (forward[level], sums, below, above),
            [solved_shape, sums_shape],
            [total],
        )
        reduced.append(latest)
    below, above = exchange(sums[2], sums[0])
    packed_shape = ((LEVELS, PAIRS, PART, 128), BF16)
    for_first, for_second = call(
        last_kernel,
        [packed_shape] * 2,
        (forward[0], sums, below, above, *reduced[::-1]),
        [VMEM(*solved_shape)],
    )
    packed = jnp.where(core == 1, for_second, lax.ppermute(for_first, "lvl", to_first))
    parts = lax.all_to_all(packed, "lvl", 0, 0, axis_index_groups=groups)
    parts = lax.ppermute(parts, AXES, to_native)
    out_shape = ((SLOTS, ORDER, COLS), BF16)
    (backward_out,) = call(finish_backward_kernel, [out_shape], (shift, parts, diag_inverse))
    forward_parts = jnp.where(stored_low, same, swapped)
    other_parts = lax.ppermute(jnp.where(stored_low, swapped, same), "lvl", to_second)
    forward_parts = jnp.where(core == 1, other_parts, forward_parts)
    (forward_out,) = call(finish_forward_kernel, [out_shape], (home, forward_parts))
    return forward_out, backward_out


def solution(mesh):
    return jax.shard_map(
        per_device,
        mesh=mesh,
        in_specs=(
            P(AXES, None, None),
            P(AXES, None, None, None),
            P(AXES, None, None),
            P(AXES, None),
        ),
        out_specs=(P(AXES, None, None), P(AXES, None, None)),
        check_vma=False,
    )
```
